256 devices in a mesh: row: 64 (over x, z, core), col: 4 (over y).
Axes of the slice: x: 4, y: 4, z: 8, core: 2. Of those that a mesh axis runs over, the one named last changes fastest.
Arguments:
- query_grads: bfloat16 [4, 8192, 28672], P(None, 'row', 'col'), may hold values from -0.00036621094 to 0.00036621094
- out_grads: bfloat16 [1024, 8192], P('col', 'row'), may hold values from -6 to 6
- activations: bfloat16 [1024, 28672], P('row', 'col'), may hold values from -6 to 6
- seq_ids: int32 [1024], P('row'), may hold values from 0 to 31, never falling along the last dimension, each value on 1 to 64 neighbouring positions
Outputs:
- scores: float32 [1024, 4], P('row')
- seq_scores: float32 [32, 4], replicated
The draws below stay inside these ranges and needn't reach their ends.
Inputs may be any that keep to these rules, and one draw needn't show every extreme that they name: `seq_ids`: non-decreasing along the tokens; every sequence holds between 1 and 64 tokens.
All inputs are finite; a program needn't handle non-finite values.
Results may differ from the reference program's by a relative error of at most 0.0003.
Values may be sent and summed in bfloat16 or wider, within the bound.
No kernel may reach another device: no remote copies, remote signals or barrier semaphores. Data moves between devices by JAX's collectives and lax.ppermute only.
A program may use at most 64 MiB of HBM per device.

```python
import math
import jax
import jax.numpy as jnp
import numpy as np
from jax import lax

D = 8192
FF = 28672
Q = 4
CAND = 1024
NSEQ = 32


def levels(stream_key, dims, cuts, low, top_value):
    def one(dim, shards_of):
        draws = jax.random.uniform(jax.random.fold_in(jax.random.fold_in(stream_key, 6), dim), (shards_of,), jnp.float32, low / len(cuts), top_value / len(cuts))
        return jnp.repeat(jnp.exp(draws), dims[dim] // shards_of).reshape((-1,) + (1,) * (len(dims) - dim - 1))

    level = one(*cuts[0])
    for cut in cuts[1:]:
        level = level * one(*cut)
    return level


def length_profile(count, total, reach, skew):
    loads = [(1 << 20) // math.isqrt(standing ** skew) + 1 for standing in range(2, count + 1)]
    spare, holding = total - reach - (count - 1), [1] * (count - 1)
    while spare > 0:
        movable = [i for i in range(count - 1) if holding[i] < reach]
        mass, remaining = sum([loads[i] for i in movable]), spare
        for i in movable:
            addition = min(reach - holding[i], max(1, remaining * loads[i] // mass), spare)
            holding[i] = holding[i] + addition
            spare = spare - addition
    return np.array([reach] + holding)


def uneven(stream_key, count, total, reach, slope):
    if count == 2:
        one = jax.random.randint(stream_key, (), max(1, total - reach), min(reach, total - 1) + 1)
        return jnp.stack([one, total - one])
    lengths = jnp.asarray(length_profile(count, total, reach, slope), jnp.int32)
    twos = (count - 1) // 2
    donor, taker = lengths[1:1 + 2 * twos:2], lengths[2:2 + 2 * twos:2]
    margin = jnp.minimum(donor - 1, reach - taker)
    shifted = jax.random.randint(jax.random.fold_in(stream_key, 1), (twos,), 0, 1 << 20) % (margin + 1)
    lengths = lengths.at[1:1 + 2 * twos:2].set(donor - shifted).at[2:2 + 2 * twos:2].set(taker + shifted)
    return lengths[jax.random.permutation(jax.random.fold_in(stream_key, 2), count)]


def bell_draw(own_key, extent, spread, limit, split=(), held_as=jnp.bfloat16):
    values = spread * jax.random.normal(own_key, extent, jnp.float32)
    if split:
        values = values * levels(own_key, extent, split, -0.22, 0.18)
    return jnp.clip(values, -limit, limit).astype(held_as)


def setup_inputs(seed: int = 0) -> dict:
    key_of = jax.random.split(jax.random.key(seed), 5)
    return {
        "query_grads": bell_draw(key_of[0], (Q, D, FF), (D * FF) ** -0.5, 0.00036621094, ((1, 64), (2, 4))),
        "out_grads": bell_draw(key_of[1], (CAND, D), 1.0, 6.0, ((0, 4), (1, 64))),
        "activations": bell_draw(key_of[2], (CAND, FF), 1.0, 6.0, ((0, 64), (1, 4))),
        "seq_ids": jnp.searchsorted(jnp.cumsum(uneven(key_of[3], NSEQ, CAND, min(64, CAND // 2), 1)), jnp.arange(CAND), side="right").astype(jnp.int32),
    }


def reference(query_grads, out_grads, activations, seq_ids):
    grads_t = out_grads.astype(jnp.float32).T

    def one_query(matrix):
        inner = jnp.dot(matrix, activations.T, preferred_element_type=jnp.float32)
        return jnp.sum(inner * grads_t, axis=0)

    scores = lax.map(one_query, query_grads).T
    onehot = (seq_ids[:, None] == jnp.arange(NSEQ, dtype=jnp.int32)[None, :]).astype(jnp.float32)
    seq_scores = jnp.dot(onehot.T, scores, precision=lax.Precision.HIGHEST)
    return scores, seq_scores
```

```python
import jax
import jax.numpy as jnp
from jax import lax
from jax.sharding import PartitionSpec as P

EXACT = lax.Precision.HIGHEST


def block_scores(flat_grads, pieces, grad_slice, queries):
    inner = jnp.dot(flat_grads, pieces.T, preferred_element_type=jnp.float32)
    inner = inner.reshape(queries, grad_slice.shape[1], pieces.shape[0])
    return jnp.einsum("qrt,tr->qt", inner, grad_slice.astype(jnp.float32))


def body(query_grads, out_grads, activations, seq_ids):
    queries, rows_here, cols_here = query_grads.shape
    rows, cols = lax.axis_size("row"), lax.axis_size("col")
    tokens_here = seq_ids.shape[0]
    flat_grads = query_grads.reshape(queries * rows_here, cols_here)
    all_acts = lax.all_gather(activations, "row", axis=0, tiled=True)
    all_grads = lax.all_gather(out_grads, "col", axis=0, tiled=True)
    copies = jnp.broadcast_to(seq_ids[None, :], (rows, tokens_here))
    all_ids = lax.all_to_all(copies, "row", 0, 0, tiled=True).reshape(-1)
    total_tokens = tokens_here * rows
    seq_count = max(total_tokens // 32, 4)
    onehot = (all_ids[:, None] == jnp.arange(seq_count, dtype=jnp.int32)[None, :]).astype(
        jnp.float32
    )
    partial = block_scores(flat_grads, all_acts, all_grads, queries)
    partial_seq = jnp.dot(partial, onehot, precision=EXACT)
    mine = partial.reshape(queries, rows, tokens_here).transpose(1, 0, 2).reshape(rows, -1)
    parts = jnp.concatenate(
        [mine, jnp.broadcast_to(partial_seq.reshape(1, -1), (rows, queries * seq_count))], axis=1
    )
    parts = jnp.broadcast_to(parts[:, None, :], (rows, cols, parts.shape[1]))
    parts = parts.reshape(rows * cols, -1)
    arrived = lax.all_to_all(parts, ("row", "col"), 0, 0, tiled=True)
    total = jnp.sum(arrived, axis=0)
    split = queries * tokens_here
    scores = total[:split].reshape(queries, tokens_here).T
    seq_scores = total[split:].reshape(queries, seq_count).T
    return (scores, seq_scores)


def solution(mesh):
    placed = (P(None, "row", "col"), P("col", "row"), P("row", "col"), P("row"))
    return jax.shard_map(
        body, mesh=mesh, in_specs=placed, out_specs=(P("row", None), P()), check_vma=False
    )
```

```python
import jax
import jax.numpy as jnp
import numpy as np
from jax import lax
from jax.sharding import PartitionSpec as P

EXACT = lax.Precision.HIGHEST
NX, NZ = 4, 8


def cat(parts, axis=0):
    return parts[0] if len(parts) == 1 else jnp.concatenate(parts, axis)


def shift(block, dx, dz):
    pairs = [
        ((x * NZ + z) * 2 + c, ((x + dx) % NX * NZ + (z + dz) % NZ) * 2 + c)
        for x in range(NX)
        for z in range(NZ)
        for c in range(2)
    ]
    return lax.ppermute(block, "row", pairs)


def swap(block):
    return lax.ppermute(block, "row", [(i, i ^ 1) for i in range(NX * NZ * 2)])


def from_col(block, ahead, cols):
    return lax.ppermute(block, "col", [(i, (i - ahead) % cols) for i in range(cols)])


L, H, F = (0,), (1,), (0, 1)
E = (1, 0), (-1, 0), (0, 1), (0, -1)
ROUNDS = [
    [(d, [((0, 0), F, d)]) for d in E],
    [
        (E[0], [((1, 0), L, (2, 0)), ((0, 1), F, (1, 1))]),
        (E[1], [((-1, 0), H, (2, 0)), ((0, -1), F, (-1, -1))]),
        (E[2], [((0, 1), F, (0, 2)), ((-1, 0), F, (-1, 1))]),
        (E[3], [((0, -1), F, (0, -2)), ((1, 0), F, (1, -1))]),
    ],
    [
        (E[0], [((1, 1), L, (2, 1)), ((1, -1), L, (2, -1)), ((0, 2), F, (1, 2))]),
        (E[1], [((-1, 1), H, (2, 1)), ((-1, -1), H, (2, -1)), ((0, -2), F, (-1, -2))]),
        (E[2], [((0, 2), F, (0, 3)), ((-1, 1), F, (-1, 2))]),
        (E[3], [((0, -2), F, (0, -3)), ((1, -1), F, (1, -2))]),
    ],
    [
        (E[0], [((1, 2), L, (2, 2)), ((1, -2), L, (2, -2)), ((0, 3), F, (1, 3))]),
        (E[1], [((-1, 2), H, (2, 2)), ((-1, -2), H, (2, -2)), ((0, -3), F, (-1, -3))]),
        (E[2], [((0, 3), L, (0, 4)), ((-1, 2), F, (-1, 3))]),
        (E[3], [((0, -3), H, (0, 4)), ((1, -2), F, (1, -3))]),
    ],
    [
        (E[0], [((1, 3), L, (2, 3)), ((1, -3), L, (2, -3))]),
        (E[1], [((-1, 3), H, (2, 3)), ((-1, -3), H, (2, -3))]),
        (E[2], [((1, 3), L, (1, 4)), ((-1, 3), L, (-1, 4))]),
        (E[3], [((1, -3), H, (1, 4)), ((-1, -3), H, (-1, 4))]),
        ((1, 1), [((1, 3), F, (2, 4))]),
    ],
]


def body(query_grads, out_grads, activations, seq_ids):
    queries, rows_here, width = query_grads.shape
    half = width // 2
    tokens = seq_ids.shape[0]
    rows, cols = lax.axis_size("row"), lax.axis_size("col")
    seq_count = max(tokens * rows // 32, 4)
    row, y = lax.axis_index("row"), lax.axis_index("col")
    core, z, x = row % 2, row // 2 % NZ, row // (2 * NZ)

    def columns(array, which):
        start = (0,) * (array.ndim - 1) + (which * half,)
        return lax.dynamic_slice(array, start, array.shape[:-1] + (half,))

    ids = jnp.broadcast_to(seq_ids[:, None].astype(activations.dtype), (tokens, 128))
    mine = cat([columns(activations, core), ids], 1)
    other = swap(cat([columns(activations, 1 - core), ids], 1))
    own = jnp.where(core == 0, cat([mine, other]), cat([other, mine]))

    grads = cat([columns(query_grads, core), swap(columns(query_grads, 1 - core))])
    grads = grads.reshape(2 * queries * rows_here, half)
    slices = cat([out_grads, swap(out_grads)], 1)
    slices = jnp.stack([slices] + [from_col(slices, k, cols) for k in range(1, cols)])
    slices = lax.dynamic_slice_in_dim(cat([slices, slices]), (x - y) % NX, NX)
    slices = slices.reshape(NX, NZ, 2, tokens, 2 * rows_here)
    slices = lax.dynamic_slice_in_dim(cat([slices, slices], 1), z, NZ, 1)

    held = {((0, 0), h): own[h * tokens : (h + 1) * tokens] for h in F}
    slots, scores, came_ids = [], [], []

    def work(arrays, places):
        block = cat(arrays)
        weights = cat([slices[-ox % NX, -oz % NZ, h] for (ox, oz), h in places])
        inner = lax.dot_general(
            grads, block[:, :half], (((1,), (1,)), ((), ())), preferred_element_type=jnp.float32
        )
        inner = inner.reshape(2, queries, rows_here, block.shape[0])
        weights = weights.astype(jnp.float32).T.reshape(2, 1, rows_here, block.shape[0])
        scores.append(jnp.sum(inner * weights, axis=(0, 2)))
        came_ids.append(block[:, half])
        slots.extend(places)

    arrays, places = [own], [((0, 0), h) for h in F]
    for moves in ROUNDS:
        came = []
        for (dx, dz), load in moves:
            sent = cat([cat([held[src, h] for h in part]) for src, part, _ in load])
            came.append((shift(sent, dx, dz), [(dst, h) for _, part, dst in load for h in part]))
        for array, names in came:
            for i, name in enumerate(names):
                held[name] = array[i * tokens : (i + 1) * tokens]
            arrays.append(array)
            places += names
        work(arrays, places)
        arrays, places = [], []

    partial = cat(scores, 1)
    all_ids = cat(came_ids).astype(jnp.int32)
    onehot = all_ids[:, None] == jnp.arange(seq_count, dtype=jnp.int32)[None, :]
    partial_seq = jnp.dot(partial, onehot.astype(jnp.float32), precision=EXACT)
    far = np.array([(NX - ox, NZ - oz, h) for (ox, oz), h in slots], np.int32).T
    owner = ((x + far[0]) % NX * NZ + (z + far[1]) % NZ) * 2 + far[2]
    place = owner[:, None] == jnp.arange(rows, dtype=jnp.int32)[None, :]
    mine = jnp.einsum(
        "qst,so->oqt",
        partial.reshape(queries, rows, tokens),
        place.astype(jnp.float32),
        precision=EXACT,
    ).reshape(rows, -1)
    parts = cat(
        [mine, jnp.broadcast_to(partial_seq.reshape(1, -1), (rows, queries * seq_count))], 1
    )
    parts = jnp.broadcast_to(parts[:, None, :], (rows, cols, parts.shape[1]))
    parts = parts.reshape(rows * cols, -1)
    arrived = lax.all_to_all(parts, ("row", "col"), 0, 0, tiled=True)
    total = jnp.sum(arrived, axis=0)
    split = queries * tokens
    scores = total[:split].reshape(queries, tokens).T
    seq_scores = total[split:].reshape(queries, seq_count).T
    return (scores, seq_scores)


def solution(mesh):
    placed = (P(None, "row", "col"), P("col", "row"), P("row", "col"), P("row"))
    return jax.shard_map(
        body, mesh=mesh, in_specs=placed, out_specs=(P("row", None), P()), check_vma=False
    )
```

```python
import functools

import jax
import jax.numpy as jnp
import numpy as np
from jax import lax
from jax.experimental import pallas as pl
from jax.experimental.pallas import tpu as pltpu
from jax.sharding import PartitionSpec as P

EXACT = lax.Precision.HIGHEST
NX, NZ = 4, 8


def cat(parts, axis=0):
    return parts[0] if len(parts) == 1 else jnp.concatenate(parts, axis)


def shift(block, dx, dz):
    pairs = [
        ((x * NZ + z) * 2 + c, ((x + dx) % NX * NZ + (z + dz) % NZ) * 2 + c)
        for x in range(NX)
        for z in range(NZ)
        for c in range(2)
    ]
    return lax.ppermute(block, "row", pairs)


def swap(block):
    return lax.ppermute(block, "row", [(i, i ^ 1) for i in range(NX * NZ * 2)])


def from_col(block, ahead, cols):
    return lax.ppermute(block, "col", [(i, (i - ahead) % cols) for i in range(cols)])


L, H, F = (0,), (1,), (0, 1)
E = (1, 0), (-1, 0), (0, 1), (0, -1)
ROUNDS = [
    [(d, [((0, 0), F, d)]) for d in E],
    [
        (E[0], [((1, 0), L, (2, 0)), ((0, 1), F, (1, 1))]),
        (E[1], [((-1, 0), H, (2, 0)), ((0, -1), F, (-1, -1))]),
        (E[2], [((0, 1), F, (0, 2)), ((-1, 0), F, (-1, 1))]),
        (E[3], [((0, -1), F, (0, -2)), ((1, 0), F, (1, -1))]),
    ],
    [
        (E[0], [((1, 1), L, (2, 1)), ((1, -1), L, (2, -1)), ((0, 2), F, (1, 2))]),
        (E[1], [((-1, 1), H, (2, 1)), ((-1, -1), H, (2, -1)), ((0, -2), F, (-1, -2))]),
        (E[2], [((0, 2), F, (0, 3)), ((-1, 1), F, (-1, 2))]),
        (E[3], [((0, -2), F, (0, -3)), ((1, -1), F, (1, -2))]),
    ],
    [
        (E[0], [((1, 2), L, (2, 2)), ((1, -2), L, (2, -2)), ((0, 3), F, (1, 3))]),
        (E[1], [((-1, 2), H, (2, 2)), ((-1, -2), H, (2, -2)), ((0, -3), F, (-1, -3))]),
        (E[2], [((0, 3), L, (0, 4)), ((-1, 2), F, (-1, 3))]),
        (E[3], [((0, -3), H, (0, 4)), ((1, -2), F, (1, -3))]),
    ],
    [
        (E[0], [((1, 3), L, (2, 3)), ((1, -3), L, (2, -3))]),
        (E[1], [((-1, 3), H, (2, 3)), ((-1, -3), H, (2, -3))]),
        (E[2], [((1, 3), L, (1, 4)), ((-1, 3), L, (-1, 4))]),
        (E[3], [((1, -3), H, (1, 4)), ((-1, -3), H, (-1, 4))]),
        ((1, 1), [((1, 3), F, (2, 4))]),
    ],
]


def scores_kernel(places, sizes, where, q_own, q_other, *refs):
    slices, pieces = refs[:NX], refs[NX : NX + len(sizes)]
    out, seq, q_buf, a_buf, g_buf, w_buf, q_sem, a_sem, g_sem = refs[NX + len(sizes) :]
    queries, rows, half = q_other.shape
    tokens = sum(sizes) // len(places)
    start = pl.multiple_of(where[2] * half, 128)
    q_copies = [
        [
            pltpu.make_async_copy(
                q_own.at[q, :, pl.ds(start, half)], q_buf.at[0, q], q_sem.at[0, q]
            )
            for q in range(queries)
        ],
        [
            pltpu.make_async_copy(q_other.at[q], q_buf.at[1, q], q_sem.at[1, q])
            for q in range(queries)
        ],
    ]
    g_copies = [
        pltpu.make_async_copy(g, g_buf.at[k], g_sem.at[k]) for k, g in enumerate(slices)
    ]
    count, a_copies = 0, []
    for i, (piece, size) in enumerate(zip(pieces, sizes)):
        a_copies.append(
            pltpu.make_async_copy(piece, a_buf.at[pl.ds(count, size)], a_sem.at[i])
        )
        count += size
    for copy in g_copies + a_copies + q_copies[0] + q_copies[1]:
        copy.start()
    for copy in g_copies:
        copy.wait()
    for i, ((ox, oz), h) in enumerate(places):
        u = lax.rem(where[0] + (NX - ox), NX)
        v = lax.rem(where[1] + (NZ - oz), NZ)
        at = pl.multiple_of(v * (2 * tokens) + h * tokens, tokens)
        w_buf[pl.ds(i * tokens, tokens)] = g_buf[u, pl.ds(at, tokens)]
    weights = w_buf[...].astype(jnp.float32).T
    for copy in a_copies:
        copy.wait()
    total = [jnp.zeros((1, count), jnp.float32) for _ in range(queries)]
    for p in range(2):
        for copy in q_copies[p]:
            copy.wait()
        inner = lax.dot_general(
            q_buf[p].reshape(queries * rows, half),
            a_buf[:, :half],
            (((1,), (1,)), ((), ())),
            preferred_element_type=jnp.float32,
        )
        for q in range(queries):
            weighed = inner[q * rows : (q + 1) * rows] * weights[p * rows : (p + 1) * rows]
            total[q] = total[q] + jnp.sum(weighed, axis=0, keepdims=True)
    scores = jnp.concatenate(total + [jnp.zeros((8 - queries, count), jnp.float32)], 0)
    out[...] = scores
    ids = a_buf[:, half:].astype(jnp.float32)
    lane = lax.broadcasted_iota(jnp.int32, (count, 128), 1).astype(jnp.float32)
    onehot = jnp.where(ids == lane, 1.0, 0.0)
    seq[...] = jnp.dot(scores, onehot, precision=EXACT, preferred_element_type=jnp.float32)


def piece_scores(where, q_own, q_other, slices, pieces, places):
    sizes = [piece.shape[0] for piece in pieces]
    count = sum(sizes)
    queries, rows, half = q_other.shape
    anywhere = pl.BlockSpec(memory_space=pl.ANY)
    whole = pl.BlockSpec(memory_space=pltpu.VMEM)
    return pl.pallas_call(
        functools.partial(scores_kernel, places, sizes),
        out_shape=(
            jax.ShapeDtypeStruct((8, count), jnp.float32),
            jax.ShapeDtypeStruct((8, 128), jnp.float32),
        ),
        in_specs=[pl.BlockSpec(memory_space=pltpu.SMEM)] + [anywhere] * (2 + NX + len(pieces)),
        out_specs=[whole, whole],
        scratch_shapes=[
            pltpu.VMEM((2, queries, rows, half), jnp.bfloat16),
            pltpu.VMEM((count, half + 128), jnp.bfloat16),
            pltpu.VMEM((NX,) + slices[0].shape, jnp.bfloat16),
            pltpu.VMEM((count, 2 * rows), jnp.bfloat16),
            pltpu.SemaphoreType.DMA((2, queries)),
            pltpu.SemaphoreType.DMA((len(pieces),)),
            pltpu.SemaphoreType.DMA((NX,)),
        ],
        compiler_params=pltpu.CompilerParams(vmem_limit_bytes=24 << 20),
        cost_estimate=pl.CostEstimate(
            flops=4 * queries * rows * half * count,
            bytes_accessed=4 * queries * rows * half + 2 * half * count,
            transcendentals=0,
        ),
        name="scores",
    )(where, q_own, q_other, *slices, *pieces)


def body(query_grads, out_grads, activations, seq_ids):
    queries, rows_here, width = query_grads.shape
    half = width // 2
    tokens = seq_ids.shape[0]
    rows, cols = lax.axis_size("row"), lax.axis_size("col")
    seq_count = max(tokens * rows // 32, 4)
    row, y = lax.axis_index("row"), lax.axis_index("col")
    core, z, x = row % 2, row // 2 % NZ, row // (2 * NZ)

    def columns(array, which):
        start = (0,) * (array.ndim - 1) + (which * half,)
        return lax.dynamic_slice(array, start, array.shape[:-1] + (half,))

    ids = jnp.broadcast_to(seq_ids[:, None].astype(activations.dtype), (tokens, 128))
    mine = cat([columns(activations, core), ids], 1)
    other = swap(cat([columns(activations, 1 - core), ids], 1))
    own = jnp.where(core == 0, cat([mine, other]), cat([other, mine]))

    own, query_grads = lax.optimization_barrier((own, query_grads))

    q_other = columns(query_grads, 1 - core)
    slices = [cat([out_grads, swap(out_grads)], 1)]
    where = jnp.stack([(x - y) % NX, z, core]).astype(jnp.int32)

    held = {((0, 0), h): own[h * tokens : (h + 1) * tokens] for h in F}
    slots, scores, by_seq = [], [], []
    arrays, places = [own], [((0, 0), h) for h in F]
    for number, moves in enumerate(ROUNDS):
        sent = [cat([cat([held[src, h] for h in part]) for src, part, _ in load]) for _, load in moves]
        if number == 1:
            sent, slices, q_other = lax.optimization_barrier((sent, slices, q_other))
            q_other = swap(q_other)
            slices += [from_col(slices[0], k, cols) for k in range(1, cols)]
        if number == 2:
            sent, slices, q_other = lax.optimization_barrier((sent, slices, q_other))
        if number > 2:
            sent, scores[-1] = lax.optimization_barrier((sent, scores[-1]))
        if number > 1:
            part, seq = piece_scores(where, query_grads, q_other, slices, arrays, places)
            scores.append(part)
            by_seq.append(seq)
            slots += places
            arrays, places = [], []
        for ((dx, dz), load), block in zip(moves, sent):
            came = shift(block, dx, dz)
            names = [(dst, h) for _, part, dst in load for h in part]
            for i, name in enumerate(names):
                held[name] = came[i * tokens : (i + 1) * tokens]
            arrays.append(came)
            places += names
    part, seq = piece_scores(where, query_grads, q_other, slices, arrays, places)
    scores.append(part)
    by_seq.append(seq)
    slots += places

    partial = cat(scores, 1)[:queries]
    partial_seq = sum(by_seq[1:], by_seq[0])[:queries, :seq_count]
    far = np.array([(NX - ox, NZ - oz, h) for (ox, oz), h in slots], np.int32).T
    owner = ((x + far[0]) % NX * NZ + (z + far[1]) % NZ) * 2 + far[2]
    place = owner[:, None] == jnp.arange(rows, dtype=jnp.int32)[None, :]
    mine = jnp.einsum(
        "qst,so->oqt",
        partial.reshape(queries, rows, tokens),
        place.astype(jnp.float32),
        precision=EXACT,
    ).reshape(rows, -1)
    parts = cat(
        [mine, jnp.broadcast_to(partial_seq.reshape(1, -1), (rows, queries * seq_count))], 1
    )
    parts = jnp.broadcast_to(parts[:, None, :], (rows, cols, parts.shape[1]))
    parts = parts.reshape(rows * cols, -1)
    arrived = lax.all_to_all(parts, ("row", "col"), 0, 0, tiled=True)
    total = jnp.sum(arrived, axis=0)
    split = queries * tokens
    scores = total[:split].reshape(queries, tokens).T
    seq_scores = total[split:].reshape(queries, seq_count).T
    return (scores, seq_scores)


def solution(mesh):
    placed = (P(None, "row", "col"), P("col", "row"), P("row", "col"), P("row"))
    return jax.shard_map(
        body, mesh=mesh, in_specs=placed, out_specs=(P("row", None), P()), check_vma=False
    )
```

```python
import functools

import jax
import jax.numpy as jnp
import numpy as np
from jax import lax
from jax.experimental import pallas as pl
from jax.experimental.pallas import tpu as pltpu
from jax.sharding import PartitionSpec as P

EXACT = lax.Precision.HIGHEST
WORK = 256
NX, NZ = 4, 8


def cat(parts, axis=0):
    return parts[0] if len(parts) == 1 else jnp.concatenate(parts, axis)


def shift(block, dx, dz):
    pairs = [
        ((x * NZ + z) * 2 + c, ((x + dx) % NX * NZ + (z + dz) % NZ) * 2 + c)
        for x in range(NX)
        for z in range(NZ)
        for c in range(2)
    ]
    return lax.ppermute(block, "row", pairs)


def swap(block):
    return lax.ppermute(block, "row", [(i, i ^ 1) for i in range(NX * NZ * 2)])


def from_col(block, ahead, cols):
    return lax.ppermute(block, "col", [(i, (i - ahead) % cols) for i in range(cols)])


L, H, F = (0,), (1,), (0, 1)
E = (1, 0), (-1, 0), (0, 1), (0, -1)
ROUNDS = [
    [(d, [((0, 0), F, d)]) for d in E],
    [
        (E[0], [((1, 0), L, (2, 0)), ((0, 1), F, (1, 1))]),
        (E[1], [((-1, 0), H, (2, 0)), ((0, -1), F, (-1, -1))]),
        (E[2], [((0, 1), F, (0, 2)), ((-1, 0), F, (-1, 1))]),
        (E[3], [((0, -1), F, (0, -2)), ((1, 0), F, (1, -1))]),
    ],
    [
        (E[0], [((1, 1), L, (2, 1)), ((1, -1), L, (2, -1)), ((0, 2), F, (1, 2))]),
        (E[1], [((-1, 1), H, (2, 1)), ((-1, -1), H, (2, -1)), ((0, -2), F, (-1, -2))]),
        (E[2], [((0, 2), F, (0, 3)), ((-1, 1), F, (-1, 2))]),
        (E[3], [((0, -2), F, (0, -3)), ((1, -1), F, (1, -2))]),
    ],
    [
        (E[0], [((1, 2), L, (2, 2)), ((1, -2), L, (2, -2)), ((0, 3), F, (1, 3))]),
        (E[1], [((-1, 2), H, (2, 2)), ((-1, -2), H, (2, -2)), ((0, -3), F, (-1, -3))]),
        (E[2], [((0, 3), L, (0, 4)), ((-1, 2), F, (-1, 3))]),
        (E[3], [((0, -3), H, (0, 4)), ((1, -2), F, (1, -3))]),
    ],
    [
        (E[0], [((1, 3), L, (2, 3)), ((1, -3), L, (2, -3))]),
        (E[1], [((-1, 3), H, (2, 3)), ((-1, -3), H, (2, -3))]),
        (E[2], [((1, 3), L, (1, 4)), ((-1, 3), L, (-1, 4))]),
        (E[3], [((1, -3), H, (1, 4)), ((-1, -3), H, (-1, 4))]),
        ((1, 1), [((1, 3), F, (2, 4))]),
    ],
]


def scores_kernel(places, sizes, where, q_own, q_other, *refs):
    slices, pieces = refs[:2], refs[2 : 2 + len(sizes)]
    out, seq, q_buf, a_buf, a_turned, g_buf, w_buf, q_sem, a_sem, g_sem = refs[2 + len(sizes) :]
    queries, rows, half = q_other.shape
    tokens = sum(sizes) // len(places)
    start = pl.multiple_of(where[2] * half, 128)
    g_copies = [
        pltpu.make_async_copy(g, g_buf.at[k], g_sem.at[k]) for k, g in enumerate(slices)
    ]
    count, a_copies = 0, []
    for i, (piece, size) in enumerate(zip(pieces, sizes)):
        a_copies.append(
            pltpu.make_async_copy(piece, a_buf.at[pl.ds(count, size)], a_sem.at[i])
        )
        count += size
    q_copies = [
        pltpu.make_async_copy(
            q_own.at[q, :, pl.ds(start, half)], q_buf.at[0, q], q_sem.at[0, q]
        )
        for q in range(queries)
    ] + [
        pltpu.make_async_copy(q_other.at[q], q_buf.at[1, q], q_sem.at[1, q])
        for q in range(queries)
    ]
    for copy in g_copies + a_copies + q_copies:
        copy.start()
    for copy in g_copies:
        copy.wait()
    for i, ((ox, oz), h) in enumerate(places):
        u = lax.rem(where[0] + (NX - ox), NX)
        v = lax.rem(where[1] + (NZ - oz), NZ)
        at = pl.multiple_of(((u % 2 * NZ + v) * 2 + h) * tokens, tokens)
        w_buf[pl.ds(i * tokens, tokens)] = g_buf[u // 2, pl.ds(at, tokens)]
    weights = w_buf[...].astype(jnp.float32).T
    for copy in a_copies:
        copy.wait()
    a_turned[...] = a_buf[:, :half].T
    total = [jnp.zeros((1, count), jnp.float32) for _ in range(queries)]
    for p in range(2):
        for q in range(queries):
            q_copies[p * queries + q].wait()
            inner = jnp.dot(q_buf[p, q], a_turned[...], preferred_element_type=jnp.float32)
            weighed = inner * weights[p * rows : (p + 1) * rows]
            total[q] = total[q] + jnp.sum(weighed, axis=0, keepdims=True)
    scores = jnp.concatenate(total + [jnp.zeros((8 - queries, count), jnp.float32)], 0)
    out[...] = scores
    ids = a_buf[:, half:].astype(jnp.float32)
    lane = lax.broadcasted_iota(jnp.int32, (count, 128), 1).astype(jnp.float32)
    onehot = jnp.where(ids == lane, 1.0, 0.0)
    seq[...] = jnp.dot(scores, onehot, precision=EXACT, preferred_element_type=jnp.float32)


def piece_scores(where, q_own, q_other, slices, pieces, places):
    sizes = [piece.shape[0] for piece in pieces]
    count = sum(sizes)
    queries, rows, half = q_other.shape
    anywhere = pl.BlockSpec(memory_space=pl.ANY)
    whole = pl.BlockSpec(memory_space=pltpu.VMEM)
    streamed = pl.BlockSpec(memory_space=pltpu.HBM)
    return pl.pallas_call(
        functools.partial(scores_kernel, places, sizes),
        out_shape=(
            jax.ShapeDtypeStruct((8, count), jnp.float32),
            jax.ShapeDtypeStruct((8, 128), jnp.float32),
        ),
        in_specs=[pl.BlockSpec(memory_space=pltpu.SMEM)]
        + [streamed] * 2
        + [anywhere] * (2 + len(pieces)),
        out_specs=[whole, whole],
        scratch_shapes=[
            pltpu.VMEM((2, queries, rows, half), jnp.bfloat16),
            pltpu.VMEM((count, half + 128), jnp.bfloat16),
            pltpu.VMEM((half, count), jnp.bfloat16),
            pltpu.VMEM((2,) + slices[0].shape, jnp.bfloat16),
            pltpu.VMEM((count, 2 * rows), jnp.bfloat16),
            pltpu.SemaphoreType.DMA((2, queries)),
            pltpu.SemaphoreType.DMA((len(pieces),)),
            pltpu.SemaphoreType.DMA((2,)),
        ],
        compiler_params=pltpu.CompilerParams(vmem_limit_bytes=24 << 20),
        cost_estimate=pl.CostEstimate(
            flops=4 * queries * rows * half * count,
            bytes_accessed=4 * queries * rows * half + 2 * half * count,
            transcendentals=0,
        ),
        name="scores",
    )(where, q_own, q_other, *slices, *pieces)


def body(query_grads, out_grads, activations, seq_ids):
    queries, rows_here, width = query_grads.shape
    half = width // 2
    tokens = seq_ids.shape[0]
    rows, cols = lax.axis_size("row"), lax.axis_size("col")
    seq_count = max(tokens * rows // 32, 4)
    row, y = lax.axis_index("row"), lax.axis_index("col")
    core, z, x = row % 2, row // 2 % NZ, row // (2 * NZ)

    def columns(array, which):
        start = (0,) * (array.ndim - 1) + (which * half,)
        return lax.dynamic_slice(array, start, array.shape[:-1] + (half,))

    ids = jnp.broadcast_to(seq_ids[:, None].astype(activations.dtype), (tokens, 128))
    mine = cat([columns(activations, core), ids], 1)
    other = swap(cat([columns(activations, 1 - core), ids], 1))
    own = jnp.where(core == 0, cat([mine, other]), cat([other, mine]))

    own, query_grads = lax.optimization_barrier((own, query_grads))

    q_other = columns(query_grads, 1 - core)
    slices = cat([out_grads, swap(out_grads)], 1)
    slices = cat([slices, from_col(slices, 1, cols)])
    where = jnp.stack([(x - y) % NX, z, core]).astype(jnp.int32)

    held = {((0, 0), h): own[h * tokens : (h + 1) * tokens] for h in F}
    slots, scores, by_seq = [], [], []
    waiting = [(own, [((0, 0), h) for h in F])]

    def work():
        count, pieces, places = 0, [], []
        while waiting and count + waiting[0][0].shape[0] <= WORK:
            piece, names = waiting.pop(0)
            pieces.append(piece)
            places.extend(names)
            count += piece.shape[0]
        part, seq = piece_scores(where, query_grads, q_other, slices, pieces, places)
        scores.append(part)
        by_seq.append(seq)
        slots.extend(places)

    for number, moves in enumerate(ROUNDS):
        sent = [cat([cat([held[src, h] for h in part]) for src, part, _ in load]) for _, load in moves]
        if number == 1:
            sent, slices, q_other = lax.optimization_barrier((sent, slices, q_other))
            q_other = swap(q_other)
            slices = [slices, from_col(slices, 2, cols)]
        if number == 2:
            sent, slices, q_other = lax.optimization_barrier((sent, slices, q_other))
        if number > 2:
            sent, scores[-1] = lax.optimization_barrier((sent, scores[-1]))
        if number > 1:
            work()
        for ((dx, dz), load), block in zip(moves, sent):
            came = shift(block, dx, dz)
            names = [(dst, h) for _, part, dst in load for h in part]
            for i, name in enumerate(names):
                held[name] = came[i * tokens : (i + 1) * tokens]
            waiting.append((came, names))
    while waiting:
        work()

    partial = cat(scores, 1)[:queries]
    partial_seq = sum(by_seq[1:], by_seq[0])[:queries, :seq_count]
    far = np.array([(NX - ox, NZ - oz, h) for (ox, oz), h in slots], np.int32).T
    owner = ((x + far[0]) % NX * NZ + (z + far[1]) % NZ) * 2 + far[2]
    place = owner[:, None] == jnp.arange(rows, dtype=jnp.int32)[None, :]
    mine = jnp.einsum(
        "qst,so->oqt",
        partial.reshape(queries, rows, tokens),
        place.astype(jnp.float32),
        precision=EXACT,
    ).reshape(rows, -1)
    parts = cat(
        [mine, jnp.broadcast_to(partial_seq.reshape(1, -1), (rows, queries * seq_count))], 1
    )
    parts = jnp.broadcast_to(parts[:, None, :], (rows, cols, parts.shape[1]))
    parts = parts.reshape(rows * cols, -1)
    arrived = lax.all_to_all(parts, ("row", "col"), 0, 0, tiled=True)
    total = jnp.sum(arrived, axis=0)
    split = queries * tokens
    scores = total[:split].reshape(queries, tokens).T
    seq_scores = total[split:].reshape(queries, seq_count).T
    return (scores, seq_scores)


def solution(mesh):
    placed = (P(None, "row", "col"), P("col", "row"), P("row", "col"), P("row"))
    return jax.shard_map(
        body, mesh=mesh, in_specs=placed, out_specs=(P("row", None), P()), check_vma=False
    )
```

```python
import functools

import jax
import jax.numpy as jnp
import numpy as np
from jax import lax
from jax.experimental import pallas as pl
from jax.experimental.pallas import tpu as pltpu
from jax.sharding import PartitionSpec as P

EXACT = lax.Precision.HIGHEST
WORK = 256
NX, NZ = 4, 8


def cat(parts, axis=0):
    return parts[0] if len(parts) == 1 else jnp.concatenate(parts, axis)


def shift(block, dx, dz):
    pairs = [
        ((x * NZ + z) * 2 + c, ((x + dx) % NX * NZ + (z + dz) % NZ) * 2 + c)
        for x in range(NX)
        for z in range(NZ)
        for c in range(2)
    ]
    return lax.ppermute(block, "row", pairs)


def swap(block):
    return lax.ppermute(block, "row", [(i, i ^ 1) for i in range(NX * NZ * 2)])


def from_col(block, ahead, cols):
    return lax.ppermute(block, "col", [(i, (i - ahead) % cols) for i in range(cols)])


L, H, F = (0,), (1,), (0, 1)
E = (1, 0), (-1, 0), (0, 1), (0, -1)
ROUNDS = [
    [(d, [((0, 0), F, d)]) for d in E],
    [
        (E[0], [((1, 0), L, (2, 0)), ((0, 1), F, (1, 1))]),
        (E[1], [((-1, 0), H, (2, 0)), ((0, -1), F, (-1, -1))]),
        (E[2], [((0, 1), F, (0, 2)), ((-1, 0), F, (-1, 1))]),
        (E[3], [((0, -1), F, (0, -2)), ((1, 0), F, (1, -1))]),
    ],
    [
        (E[0], [((1, 1), L, (2, 1)), ((1, -1), L, (2, -1)), ((0, 2), F, (1, 2))]),
        (E[1], [((-1, 1), H, (2, 1)), ((-1, -1), H, (2, -1)), ((0, -2), F, (-1, -2))]),
        (E[2], [((0, 2), F, (0, 3)), ((-1, 1), F, (-1, 2))]),
        (E[3], [((0, -2), F, (0, -3)), ((1, -1), F, (1, -2))]),
    ],
    [
        (E[0], [((1, 2), L, (2, 2)), ((1, -2), L, (2, -2)), ((0, 3), F, (1, 3))]),
        (E[1], [((-1, 2), H, (2, 2)), ((-1, -2), H, (2, -2)), ((0, -3), F, (-1, -3))]),
        (E[2], [((0, 3), L, (0, 4)), ((-1, 2), F, (-1, 3))]),
        (E[3], [((0, -3), H, (0, 4)), ((1, -2), F, (1, -3))]),
    ],
    [
        (E[0], [((1, 3), L, (2, 3)), ((1, -3), L, (2, -3))]),
        (E[1], [((-1, 3), H, (2, 3)), ((-1, -3), H, (2, -3))]),
        (E[2], [((1, 3), L, (1, 4)), ((-1, 3), L, (-1, 4))]),
        (E[3], [((1, -3), H, (1, 4)), ((-1, -3), H, (-1, 4))]),
        ((1, 1), [((1, 3), F, (2, 4))]),
    ],
]


def scores_kernel(places, sizes, where, q_mine, q_other, *refs):
    slices, pieces = refs[:2], refs[2 : 2 + len(sizes)]
    out, seq, a_buf, g_buf, w_buf, a_sem, g_sem = refs[2 + len(sizes) :]
    queries, rows, half = q_other.shape
    tokens = sum(sizes) // len(places)
    g_copies = [
        pltpu.make_async_copy(g, g_buf.at[k], g_sem.at[k]) for k, g in enumerate(slices)
    ]
    count, a_copies = 0, []
    for i, (piece, size) in enumerate(zip(pieces, sizes)):
        a_copies.append(
            pltpu.make_async_copy(piece, a_buf.at[pl.ds(count, size)], a_sem.at[i])
        )
        count += size
    for copy in g_copies + a_copies:
        copy.start()
    for copy in g_copies:
        copy.wait()
    for i, ((ox, oz), h) in enumerate(places):
        u = lax.rem(where[0] + (NX - ox), NX)
        v = lax.rem(where[1] + (NZ - oz), NZ)
        at = pl.multiple_of(((u % 2 * NZ + v) * 2 + h) * tokens, tokens)
        w_buf[pl.ds(i * tokens, tokens)] = g_buf[u // 2, pl.ds(at, tokens)]
    weights = w_buf[...].astype(jnp.float32).T
    for copy in a_copies:
        copy.wait()
    total = [jnp.zeros((1, count), jnp.float32) for _ in range(queries)]
    for p, grads in enumerate((q_mine, q_other)):
        inner = lax.dot_general(
            grads[...].reshape(queries * rows, half),
            a_buf[:, :half],
            (((1,), (1,)), ((), ())),
            preferred_element_type=jnp.float32,
        )
        for q in range(queries):
            weighed = inner[q * rows : (q + 1) * rows] * weights[p * rows : (p + 1) * rows]
            total[q] = total[q] + jnp.sum(weighed, axis=0, keepdims=True)
    scores = jnp.concatenate(total + [jnp.zeros((8 - queries, count), jnp.float32)], 0)
    out[...] = scores
    ids = a_buf[:, half:].astype(jnp.float32)
    lane = lax.broadcasted_iota(jnp.int32, (count, 128), 1).astype(jnp.float32)
    onehot = jnp.where(ids == lane, 1.0, 0.0)
    seq[...] = jnp.dot(scores, onehot, precision=EXACT, preferred_element_type=jnp.float32)


def piece_scores(where, q_mine, q_other, slices, pieces, places):
    sizes = [piece.shape[0] for piece in pieces]
    count = sum(sizes)
    queries, rows, half = q_other.shape
    anywhere = pl.BlockSpec(memory_space=pl.ANY)
    whole = pl.BlockSpec(memory_space=pltpu.VMEM)
    return pl.pallas_call(
        functools.partial(scores_kernel, places, sizes),
        out_shape=(
            jax.ShapeDtypeStruct((8, count), jnp.float32),
            jax.ShapeDtypeStruct((8, 128), jnp.float32),
        ),
        in_specs=[pl.BlockSpec(memory_space=pltpu.SMEM)]
        + [whole] * 2
        + [anywhere] * (2 + len(pieces)),
        out_specs=[whole, whole],
        scratch_shapes=[
            pltpu.VMEM((count, half + 128), jnp.bfloat16),
            pltpu.VMEM((2,) + slices[0].shape, jnp.bfloat16),
            pltpu.VMEM((count, 2 * rows), jnp.bfloat16),
            pltpu.SemaphoreType.DMA((len(pieces),)),
            pltpu.SemaphoreType.DMA((2,)),
        ],
        compiler_params=pltpu.CompilerParams(vmem_limit_bytes=16 << 20),
        cost_estimate=pl.CostEstimate(
            flops=4 * queries * rows * half * count,
            bytes_accessed=4 * queries * rows * half + 2 * half * count,
            transcendentals=0,
        ),
        name="scores",
    )(where, q_mine, q_other, *slices, *pieces)


def body(query_grads, out_grads, activations, seq_ids):
    queries, rows_here, width = query_grads.shape
    half = width // 2
    tokens = seq_ids.shape[0]
    rows, cols = lax.axis_size("row"), lax.axis_size("col")
    seq_count = max(tokens * rows // 32, 4)
    row, y = lax.axis_index("row"), lax.axis_index("col")
    core, z, x = lax.rem(row, 2), lax.rem(lax.div(row, 2), NZ), lax.div(row, 2 * NZ)
    where = jnp.stack([lax.rem(x + cols - y, NX), z])

    def columns(array, which):
        start = (0,) * (array.ndim - 1) + (which * half,)
        return lax.dynamic_slice(array, start, array.shape[:-1] + (half,))

    ids = jnp.broadcast_to(seq_ids[:, None].astype(activations.dtype), (tokens, 128))
    mine = cat([columns(activations, core), ids], 1)
    other = swap(cat([columns(activations, 1 - core), ids], 1))
    own = jnp.where(core == 0, cat([mine, other]), cat([other, mine]))

    own, where, query_grads = lax.optimization_barrier((own, where, query_grads))

    q_other = columns(query_grads, 1 - core)
    slices = cat([out_grads, swap(out_grads)], 1)
    slices, _ = lax.optimization_barrier((slices, own))
    slices = cat([slices, from_col(slices, 1, cols)])

    held = {((0, 0), h): own[h * tokens : (h + 1) * tokens] for h in F}
    slots, scores, by_seq = [], [], []
    waiting = [(own, [((0, 0), h) for h in F])]

    def work():
        count, pieces, places = 0, [], []
        while waiting and count + waiting[0][0].shape[0] <= WORK:
            piece, names = waiting.pop(0)
            pieces.append(piece)
            places.extend(names)
            count += piece.shape[0]
        part, seq = piece_scores(where, q_mine, q_other, slices, pieces, places)
        scores.append(part)
        by_seq.append(seq)
        slots.extend(places)

    for number, moves in enumerate(ROUNDS):
        sent = [cat([cat([held[src, h] for h in part]) for src, part, _ in load]) for _, load in moves]
        if number == 1:
            sent, slices, q_other, query_grads = lax.optimization_barrier(
                (sent, slices, q_other, query_grads)
            )
            q_other, q_mine = swap(q_other), columns(query_grads, core)
        if number == 2:
            sent, slices, q_other, q_mine = lax.optimization_barrier(
                (sent, slices, q_other, q_mine)
            )
            slices = [slices, from_col(slices, 2, cols)]
        if number > 2:
            sent, scores[-1] = lax.optimization_barrier((sent, scores[-1]))
        if number > 1:
            work()
        for ((dx, dz), load), block in zip(moves, sent):
            came = shift(block, dx, dz)
            names = [(dst, h) for _, part, dst in load for h in part]
            for i, name in enumerate(names):
                held[name] = came[i * tokens : (i + 1) * tokens]
            waiting.append((came, names))
    while waiting:
        work()

    partial = cat(scores, 1)[:queries]
    partial_seq = sum(by_seq[1:], by_seq[0])[:queries, :seq_count]
    far = np.array([(NX - ox, NZ - oz, h) for (ox, oz), h in slots], np.int32).T
    owner = (lax.rem(x + far[0], NX) * NZ + lax.rem(z + far[1], NZ)) * 2 + far[2]
    place = owner[:, None] == jnp.arange(rows, dtype=jnp.int32)[None, :]
    mine = jnp.einsum(
        "qst,so->oqt",
        partial.reshape(queries, rows, tokens),
        place.astype(jnp.float32),
        precision=EXACT,
    ).reshape(rows, -1)
    parts = cat(
        [mine, jnp.broadcast_to(partial_seq.reshape(1, -1), (rows, queries * seq_count))], 1
    )
    parts = jnp.broadcast_to(parts[:, None, :], (rows, cols, parts.shape[1]))
    parts = parts.reshape(rows * cols, -1)
    arrived = lax.all_to_all(parts, ("row", "col"), 0, 0, tiled=True)
    total = jnp.sum(arrived, axis=0)
    split = queries * tokens
    scores = total[:split].reshape(queries, tokens).T
    seq_scores = total[split:].reshape(queries, seq_count).T
    return (scores, seq_scores)


def solution(mesh):
    placed = (P(None, "row", "col"), P("col", "row"), P("row", "col"), P("row"))
    return jax.shard_map(
        body, mesh=mesh, in_specs=placed, out_specs=(P("row", None), P()), check_vma=False
    )
```

```python
import functools

import jax
import jax.numpy as jnp
import numpy as np
from jax import lax
from jax.experimental import pallas as pl
from jax.experimental.pallas import tpu as pltpu
from jax.sharding import PartitionSpec as P

EXACT = lax.Precision.HIGHEST
WORK = 256
NX, NZ = 4, 8


def cat(parts, axis=0):
    return parts[0] if len(parts) == 1 else jnp.concatenate(parts, axis)


def shift(block, dx, dz):
    pairs = [
        ((x * NZ + z) * 2 + c, ((x + dx) % NX * NZ + (z + dz) % NZ) * 2 + c)
        for x in range(NX)
        for z in range(NZ)
        for c in range(2)
    ]
    return lax.ppermute(block, "row", pairs)


def swap(block):
    return lax.ppermute(block, "row", [(i, i ^ 1) for i in range(NX * NZ * 2)])


def from_col(block, ahead, cols):
    return lax.ppermute(block, "col", [(i, (i - ahead) % cols) for i in range(cols)])


L, H, F = (0,), (1,), (0, 1)
E = (1, 0), (-1, 0), (0, 1), (0, -1)
ROUNDS = [
    [(d, [((0, 0), F, d)]) for d in E],
    [
        (E[0], [((1, 0), L, (2, 0)), ((0, 1), F, (1, 1))]),
        (E[1], [((-1, 0), H, (2, 0)), ((0, -1), F, (-1, -1))]),
        (E[2], [((0, 1), F, (0, 2)), ((-1, 0), F, (-1, 1))]),
        (E[3], [((0, -1), F, (0, -2)), ((1, 0), F, (1, -1))]),
    ],
    [
        (E[0], [((1, 1), L, (2, 1)), ((1, -1), L, (2, -1)), ((0, 2), F, (1, 2))]),
        (E[1], [((-1, 1), H, (2, 1)), ((-1, -1), H, (2, -1)), ((0, -2), F, (-1, -2))]),
        (E[2], [((0, 2), F, (0, 3)), ((-1, 1), F, (-1, 2))]),
        (E[3], [((0, -2), F, (0, -3)), ((1, -1), F, (1, -2))]),
    ],
    [
        (E[0], [((1, 2), L, (2, 2)), ((1, -2), L, (2, -2)), ((0, 3), F, (1, 3))]),
        (E[1], [((-1, 2), H, (2, 2)), ((-1, -2), H, (2, -2)), ((0, -3), F, (-1, -3))]),
        (E[2], [((0, 3), L, (0, 4)), ((-1, 2), F, (-1, 3))]),
        (E[3], [((0, -3), H, (0, 4)), ((1, -2), F, (1, -3))]),
    ],
    [
        (E[0], [((1, 3), L, (2, 3)), ((1, -3), L, (2, -3))]),
        (E[1], [((-1, 3), H, (2, 3)), ((-1, -3), H, (2, -3))]),
        (E[2], [((1, 3), L, (1, 4)), ((-1, 3), L, (-1, 4))]),
        (E[3], [((1, -3), H, (1, 4)), ((-1, -3), H, (-1, 4))]),
        ((1, 1), [((1, 3), F, (2, 4))]),
    ],
]


def scores_kernel(places, sizes, where, q_mine, q_other, *refs):
    slices, pieces = refs[:2], refs[2 : 2 + len(sizes)]
    out, seq, a_buf, g_buf, w_buf, a_sem, g_sem = refs[2 + len(sizes) :]
    queries, rows, half = q_other.shape
    tokens = sum(sizes) // len(places)
    g_copies = [
        pltpu.make_async_copy(g, g_buf.at[k], g_sem.at[k]) for k, g in enumerate(slices)
    ]
    count, a_copies = 0, []
    for i, (piece, size) in enumerate(zip(pieces, sizes)):
        a_copies.append(
            pltpu.make_async_copy(piece, a_buf.at[pl.ds(count, size)], a_sem.at[i])
        )
        count += size
    for copy in g_copies + a_copies:
        copy.start()
    for copy in g_copies:
        copy.wait()
    for i, ((ox, oz), h) in enumerate(places):
        u = lax.rem(where[0] + (NX - ox), NX)
        v = lax.rem(where[1] + (NZ - oz), NZ)
        at = pl.multiple_of(((u % 2 * NZ + v) * 2 + h) * tokens, tokens)
        w_buf[pl.ds(i * tokens, tokens)] = g_buf[u // 2, pl.ds(at, tokens)]
    weights = w_buf[...].astype(jnp.float32).T
    for copy in a_copies:
        copy.wait()
    total = [jnp.zeros((1, count), jnp.float32) for _ in range(queries)]
    for p, grads in enumerate((q_mine, q_other)):
        inner = lax.dot_general(
            grads[...].reshape(queries * rows, half),
            a_buf[:, :half],
            (((1,), (1,)), ((), ())),
            preferred_element_type=jnp.float32,
        )
        for q in range(queries):
            weighed = inner[q * rows : (q + 1) * rows] * weights[p * rows : (p + 1) * rows]
            total[q] = total[q] + jnp.sum(weighed, axis=0, keepdims=True)
    scores = jnp.concatenate(total + [jnp.zeros((8 - queries, count), jnp.float32)], 0)
    out[...] = scores
    ids = a_buf[:, half:].astype(jnp.float32)
    lane = lax.broadcasted_iota(jnp.int32, (count, 128), 1).astype(jnp.float32)
    onehot = jnp.where(ids == lane, 1.0, 0.0)
    seq[...] = jnp.dot(scores, onehot, precision=EXACT, preferred_element_type=jnp.float32)


def piece_scores(where, q_mine, q_other, slices, pieces, places):
    sizes = [piece.shape[0] for piece in pieces]
    count = sum(sizes)
    queries, rows, half = q_other.shape
    anywhere = pl.BlockSpec(memory_space=pl.ANY)
    whole = pl.BlockSpec(memory_space=pltpu.VMEM)
    return pl.pallas_call(
        functools.partial(scores_kernel, places, sizes),
        out_shape=(
            jax.ShapeDtypeStruct((8, count), jnp.float32),
            jax.ShapeDtypeStruct((8, 128), jnp.float32),
        ),
        in_specs=[pl.BlockSpec(memory_space=pltpu.SMEM)]
        + [whole] * 2
        + [anywhere] * (2 + len(pieces)),
        out_specs=[whole, whole],
        scratch_shapes=[
            pltpu.VMEM((count, half + 128), jnp.bfloat16),
            pltpu.VMEM((2,) + slices[0].shape, jnp.bfloat16),
            pltpu.VMEM((count, 2 * rows), jnp.bfloat16),
            pltpu.SemaphoreType.DMA((len(pieces),)),
            pltpu.SemaphoreType.DMA((2,)),
        ],
        compiler_params=pltpu.CompilerParams(vmem_limit_bytes=16 << 20),
        cost_estimate=pl.CostEstimate(
            flops=4 * queries * rows * half * count,
            bytes_accessed=4 * queries * rows * half + 2 * half * count,
            transcendentals=0,
        ),
        name="scores",
    )(where, q_mine, q_other, *slices, *pieces)


def body(query_grads, out_grads, activations, seq_ids):
    queries, rows_here, width = query_grads.shape
    half = width // 2
    tokens = seq_ids.shape[0]
    rows, cols = lax.axis_size("row"), lax.axis_size("col")
    seq_count = max(tokens * rows // 32, 4)
    row, y = lax.axis_index("row"), lax.axis_index("col")
    core, z, x = lax.rem(row, 2), lax.rem(lax.div(row, 2), NZ), lax.div(row, 2 * NZ)
    where = jnp.stack([lax.rem(x + cols - y, NX), z])

    def columns(array, which):
        start = (0,) * (array.ndim - 1) + (which * half,)
        return lax.dynamic_slice(array, start, array.shape[:-1] + (half,))

    ids = jnp.broadcast_to(seq_ids[:, None], (tokens, 128)).astype(activations.dtype)
    mine = cat([columns(activations, core), ids], 1)
    other = swap(cat([columns(activations, 1 - core), ids], 1))
    own = jnp.where(core == 0, cat([mine, other]), cat([other, mine]))

    own, where, query_grads = lax.optimization_barrier((own, where, query_grads))

    q_slice = columns(query_grads, 1 - core)
    slices = cat([out_grads, swap(out_grads)], 1)
    slices, _ = lax.optimization_barrier((slices, own))
    slices = cat([slices, from_col(slices, 1, cols)])

    held = {((0, 0), h): own[h * tokens : (h + 1) * tokens] for h in F}
    slots, scores, by_seq = [], [], []
    waiting = [(own, [((0, 0), h) for h in F])]

    def work():
        count, pieces, places = 0, [], []
        while waiting and count + waiting[0][0].shape[0] <= WORK:
            piece, names = waiting.pop(0)
            pieces.append(piece)
            places.extend(names)
            count += piece.shape[0]
        part, seq = piece_scores(where, q_mine, q_other, slices, pieces, places)
        scores.append(part)
        by_seq.append(seq)
        slots.extend(places)

    for number, moves in enumerate(ROUNDS):
        sent = [cat([cat([held[src, h] for h in part]) for src, part, _ in load]) for _, load in moves]
        if number == 1:
            sent, slices, q_slice, query_grads = lax.optimization_barrier(
                (sent, slices, q_slice, query_grads)
            )
            slices, q_mine = [slices, from_col(slices, 2, cols)], columns(query_grads, core)
        if number == 2:
            sent, slices, q_slice, q_mine = lax.optimization_barrier(
                (sent, slices, q_slice, q_mine)
            )
            q_other = swap(q_slice)
        if number == 3:
            sent, slices, q_other = lax.optimization_barrier((sent, slices, q_other))
            work()
            work()
        if number == 4:
            sent, scores = lax.optimization_barrier((sent, scores))
            work()
        for ((dx, dz), load), block in zip(moves, sent):
            came = shift(block, dx, dz)
            names = [(dst, h) for _, part, dst in load for h in part]
            for i, name in enumerate(names):
                held[name] = came[i * tokens : (i + 1) * tokens]
            waiting.append((came, names))
    while waiting:
        work()

    partial = cat(scores, 1)[:queries]
    partial_seq = sum(by_seq[1:], by_seq[0])[:queries, :seq_count]
    far = np.array([(NX - ox, NZ - oz, h) for (ox, oz), h in slots], np.int32).T
    owner = (lax.rem(x + far[0], NX) * NZ + lax.rem(z + far[1], NZ)) * 2 + far[2]
    place = owner[:, None] == jnp.arange(rows, dtype=jnp.int32)[None, :]
    mine = jnp.einsum(
        "qst,so->oqt",
        partial.reshape(queries, rows, tokens),
        place.astype(jnp.float32),
        precision=EXACT,
    ).reshape(rows, -1)
    parts = cat(
        [mine, jnp.broadcast_to(partial_seq.reshape(1, -1), (rows, queries * seq_count))], 1
    )
    parts = jnp.broadcast_to(parts[:, None, :], (rows, cols, parts.shape[1]))
    parts = parts.reshape(rows * cols, -1)
    arrived = lax.all_to_all(parts, ("row", "col"), 0, 0, tiled=True)
    total = jnp.sum(arrived, axis=0)
    split = queries * tokens
    scores = total[:split].reshape(queries, tokens).T
    seq_scores = total[split:].reshape(queries, seq_count).T
    return (scores, seq_scores)


def solution(mesh):
    placed = (P(None, "row", "col"), P("col", "row"), P("row", "col"), P("row"))
    return jax.shard_map(
        body, mesh=mesh, in_specs=placed, out_specs=(P("row", None), P()), check_vma=False
    )
```

```python
import functools

import jax
import jax.numpy as jnp
import numpy as np
from jax import lax
from jax.experimental import pallas as pl
from jax.experimental.pallas import tpu as pltpu
from jax.sharding import PartitionSpec as P

EXACT = lax.Precision.HIGHEST
WORK = 256
NX, NZ = 4, 8


def cat(parts, axis=0):
    return parts[0] if len(parts) == 1 else jnp.concatenate(parts, axis)


def shift(block, dx, dz):
    pairs = [
        ((x * NZ + z) * 2 + c, ((x + dx) % NX * NZ + (z + dz) % NZ) * 2 + c)
        for x in range(NX)
        for z in range(NZ)
        for c in range(2)
    ]
    return lax.ppermute(block, "row", pairs)


def swap(block):
    return lax.ppermute(block, "row", [(i, i ^ 1) for i in range(NX * NZ * 2)])


def from_col(block, ahead, cols):
    return lax.ppermute(block, "col", [(i, (i - ahead) % cols) for i in range(cols)])


L, H, F = (0,), (1,), (0, 1)
E = (1, 0), (-1, 0), (0, 1), (0, -1)
ROUNDS = [
    [(d, [((0, 0), F, d)]) for d in E],
    [
        (E[0], [((1, 0), L, (2, 0)), ((0, 1), F, (1, 1))]),
        (E[1], [((-1, 0), H, (2, 0)), ((0, -1), F, (-1, -1))]),
        (E[2], [((0, 1), F, (0, 2)), ((-1, 0), F, (-1, 1))]),
        (E[3], [((0, -1), F, (0, -2)), ((1, 0), F, (1, -1))]),
    ],
    [
        (E[0], [((1, 1), L, (2, 1)), ((1, -1), L, (2, -1)), ((0, 2), F, (1, 2))]),
        (E[1], [((-1, 1), H, (2, 1)), ((-1, -1), H, (2, -1)), ((0, -2), F, (-1, -2))]),
        (E[2], [((0, 2), F, (0, 3)), ((-1, 1), F, (-1, 2))]),
        (E[3], [((0, -2), F, (0, -3)), ((1, -1), F, (1, -2))]),
    ],
    [
        (E[0], [((1, 2), L, (2, 2)), ((1, -2), L, (2, -2)), ((0, 3), F, (1, 3))]),
        (E[1], [((-1, 2), H, (2, 2)), ((-1, -2), H, (2, -2)), ((0, -3), F, (-1, -3))]),
        (E[2], [((0, 3), L, (0, 4)), ((-1, 2), F, (-1, 3))]),
        (E[3], [((0, -3), H, (0, 4)), ((1, -2), F, (1, -3))]),
    ],
    [
        (E[0], [((1, 3), L, (2, 3)), ((1, -3), L, (2, -3))]),
        (E[1], [((-1, 3), H, (2, 3)), ((-1, -3), H, (2, -3))]),
        (E[2], [((1, 3), L, (1, 4)), ((-1, 3), L, (-1, 4))]),
        (E[3], [((1, -3), H, (1, 4)), ((-1, -3), H, (-1, 4))]),
        ((1, 1), [((1, 3), F, (2, 4))]),
    ],
]


def weights_kernel(names, where, mine, ahead, *refs):
    outs, rows = refs[:-1], refs[-1]
    tokens = rows.shape[0] // len(names)
    for i, ((ox, oz), h) in enumerate(names):
        u = lax.rem(where[0] + (NX - ox), NX)
        v = lax.rem(where[1] + (NZ - oz), NZ)
        at = pl.multiple_of(((u % 2 * NZ + v) * 2 + h) * tokens, tokens)
        for k, half in enumerate((mine, ahead)):

            @pl.when(u // 2 == k)
            def _():
                rows[pl.ds(i * tokens, tokens)] = half[pl.ds(at, tokens)]

    for k, out in enumerate(outs):
        out[...] = rows[k * WORK : (k + 1) * WORK].astype(jnp.float32).T


def turned_weights(where, slices, names, tokens):
    whole = pl.BlockSpec(memory_space=pltpu.VMEM)
    count, width = len(names) * tokens, slices[0].shape[1]
    results = count // WORK
    return pl.pallas_call(
        functools.partial(weights_kernel, names),
        out_shape=[jax.ShapeDtypeStruct((width, WORK), jnp.float32)] * results,
        in_specs=[pl.BlockSpec(memory_space=pltpu.SMEM), whole, whole],
        out_specs=[whole] * results,
        scratch_shapes=[pltpu.VMEM((count, width), jnp.bfloat16)],
        compiler_params=pltpu.CompilerParams(vmem_limit_bytes=16 << 20),
        name="weights",
    )(where, *slices)


def scores_kernel(sizes, q_mine, q_other, weights, *refs):
    pieces = refs[: len(sizes)]
    out, seq, a_buf, a_sem = refs[len(sizes) :]
    queries, rows, half = q_other.shape
    count, a_copies = 0, []
    for i, (piece, size) in enumerate(zip(pieces, sizes)):
        a_copies.append(
            pltpu.make_async_copy(piece, a_buf.at[pl.ds(count, size)], a_sem.at[i])
        )
        count += size
    for copy in a_copies:
        copy.start()
    for copy in a_copies:
        copy.wait()
    total = [jnp.zeros((1, count), jnp.float32) for _ in range(queries)]
    for p, grads in enumerate((q_mine, q_other)):
        inner = lax.dot_general(
            grads[...].reshape(queries * rows, half),
            a_buf[:, :half],
            (((1,), (1,)), ((), ())),
            preferred_element_type=jnp.float32,
        )
        for q in range(queries):
            weighed = inner[q * rows : (q + 1) * rows] * weights[p * rows : (p + 1) * rows]
            total[q] = total[q] + jnp.sum(weighed, axis=0, keepdims=True)
    scores = jnp.concatenate(total + [jnp.zeros((8 - queries, count), jnp.float32)], 0)
    out[...] = scores
    ids = a_buf[:, half:].astype(jnp.float32)
    lane = lax.broadcasted_iota(jnp.int32, (count, 128), 1).astype(jnp.float32)
    onehot = jnp.where(ids == lane, 1.0, 0.0)
    seq[...] = jnp.dot(scores, onehot, precision=EXACT, preferred_element_type=jnp.float32)


def piece_scores(q_mine, q_other, weights, pieces):
    sizes = [piece.shape[0] for piece in pieces]
    count = sum(sizes)
    queries, rows, half = q_other.shape
    anywhere = pl.BlockSpec(memory_space=pl.ANY)
    whole = pl.BlockSpec(memory_space=pltpu.VMEM)
    return pl.pallas_call(
        functools.partial(scores_kernel, sizes),
        out_shape=(
            jax.ShapeDtypeStruct((8, count), jnp.float32),
            jax.ShapeDtypeStruct((8, 128), jnp.float32),
        ),
        in_specs=[whole] * 3 + [anywhere] * len(pieces),
        out_specs=[whole, whole],
        scratch_shapes=[
            pltpu.VMEM((count, half + 128), jnp.bfloat16),
            pltpu.SemaphoreType.DMA((len(pieces),)),
        ],
        compiler_params=pltpu.CompilerParams(vmem_limit_bytes=16 << 20),
        cost_estimate=pl.CostEstimate(
            flops=4 * queries * rows * half * count,
            bytes_accessed=4 * queries * rows * half + 2 * half * count,
            transcendentals=0,
        ),
        name="scores",
    )(q_mine, q_other, weights, *pieces)


def body(query_grads, out_grads, activations, seq_ids):
    queries, rows_here, width = query_grads.shape
    half = width // 2
    tokens = seq_ids.shape[0]
    rows, cols = lax.axis_size("row"), lax.axis_size("col")
    seq_count = max(tokens * rows // 32, 4)
    row, y = lax.axis_index("row"), lax.axis_index("col")
    core, z, x = lax.rem(row, 2), lax.rem(lax.div(row, 2), NZ), lax.div(row, 2 * NZ)
    where = jnp.stack([lax.rem(x + cols - y, NX), z])

    def columns(array, which):
        start = (0,) * (array.ndim - 1) + (which * half,)
        return lax.dynamic_slice(array, start, array.shape[:-1] + (half,))

    ids = jnp.broadcast_to(seq_ids[:, None], (tokens, 128)).astype(activations.dtype)
    mine = cat([columns(activations, core), ids], 1)
    other = swap(cat([columns(activations, 1 - core), ids], 1))
    own = jnp.where(core == 0, cat([mine, other]), cat([other, mine]))

    own, where, query_grads = lax.optimization_barrier((own, where, query_grads))

    q_slice = columns(query_grads, 1 - core)
    slices = cat([out_grads, swap(out_grads)], 1)
    slices, _ = lax.optimization_barrier((slices, own))
    slices = cat([slices, from_col(slices, 1, cols)])

    held = {((0, 0), h): own[h * tokens : (h + 1) * tokens] for h in F}
    order = [((0, 0), h) for h in F]
    order += [(dst, h) for moves in ROUNDS for _, load in moves for _, part, dst in load for h in part]
    slots, scores, by_seq = [], [], []
    waiting = [(own, [((0, 0), h) for h in F])]

    def work():
        count, pieces, places = 0, [], []
        while waiting and count + waiting[0][0].shape[0] <= WORK:
            piece, names = waiting.pop(0)
            pieces.append(piece)
            places.extend(names)
            count += piece.shape[0]
        part, seq = piece_scores(q_mine, q_other, weights[len(scores)], pieces)
        scores.append(part)
        by_seq.append(seq)
        slots.extend(places)

    for number, moves in enumerate(ROUNDS):
        sent = [cat([cat([held[src, h] for h in part]) for src, part, _ in load]) for _, load in moves]
        if number == 1:
            sent, slices, q_slice, query_grads = lax.optimization_barrier(
                (sent, slices, q_slice, query_grads)
            )
            slices, q_mine = [slices, from_col(slices, 2, cols)], columns(query_grads, core)
        if number == 2:
            sent, slices, q_slice, q_mine = lax.optimization_barrier(
                (sent, slices, q_slice, q_mine)
            )
            q_other = swap(q_slice)
            weights = turned_weights(where, slices, order, tokens)
        if number == 3:
            sent, weights, q_other = lax.optimization_barrier((sent, weights, q_other))
            work()
            work()
        if number == 4:
            sent, scores = lax.optimization_barrier((sent, scores))
            work()
        for ((dx, dz), load), block in zip(moves, sent):
            came = shift(block, dx, dz)
            names = [(dst, h) for _, part, dst in load for h in part]
            for i, name in enumerate(names):
                held[name] = came[i * tokens : (i + 1) * tokens]
            waiting.append((came, names))
    while waiting:
        work()

    partial = cat(scores, 1)[:queries]
    partial_seq = sum(by_seq[1:], by_seq[0])[:queries, :seq_count]
    far = np.array([(NX - ox, NZ - oz, h) for (ox, oz), h in slots], np.int32).T
    owner = (lax.rem(x + far[0], NX) * NZ + lax.rem(z + far[1], NZ)) * 2 + far[2]
    place = owner[:, None] == jnp.arange(rows, dtype=jnp.int32)[None, :]
    mine = jnp.einsum(
        "qst,so->oqt",
        partial.reshape(queries, rows, tokens),
        place.astype(jnp.float32),
        precision=EXACT,
    ).reshape(rows, -1)
    parts = cat(
        [mine, jnp.broadcast_to(partial_seq.reshape(1, -1), (rows, queries * seq_count))], 1
    )
    parts = jnp.broadcast_to(parts[:, None, :], (rows, cols, parts.shape[1]))
    parts = parts.reshape(rows * cols, -1)
    arrived = lax.all_to_all(parts, ("row", "col"), 0, 0, tiled=True)
    total = jnp.sum(arrived, axis=0)
    split = queries * tokens
    scores = total[:split].reshape(queries, tokens).T
    seq_scores = total[split:].reshape(queries, seq_count).T
    return (scores, seq_scores)


def solution(mesh):
    placed = (P(None, "row", "col"), P("col", "row"), P("row", "col"), P("row"))
    return jax.shard_map(
        body, mesh=mesh, in_specs=placed, out_specs=(P("row", None), P()), check_vma=False
    )
```

```python
import functools

import jax
import jax.numpy as jnp
import numpy as np
from jax import lax
from jax.experimental import pallas as pl
from jax.experimental.pallas import tpu as pltpu
from jax.sharding import PartitionSpec as P

EXACT = lax.Precision.HIGHEST
WORK = 256
NX, NZ = 4, 8


def cat(parts, axis=0):
    return parts[0] if len(parts) == 1 else jnp.concatenate(parts, axis)


def shift(block, dx, dz, turn=1):
    pairs = [
        (
            (x * NZ + z) * 2 + c,
            ((x + dx * turn**c) % NX * NZ + (z + dz * turn**c) % NZ) * 2 + c,
        )
        for x in range(NX)
        for z in range(NZ)
        for c in range(2)
    ]
    return lax.ppermute(block, "row", pairs)


def swap(block):
    return lax.ppermute(block, "row", [(i, i ^ 1) for i in range(NX * NZ * 2)])


def from_col(block, ahead, cols):
    return lax.ppermute(block, "col", [(i, (i - ahead) % cols) for i in range(cols)])


L, H, F = (0,), (1,), (0, 1)
E = (1, 0), (-1, 0), (0, 1), (0, -1)
ROUNDS = [
    [(d, [((0, 0), F, d)]) for d in E],
    [
        (E[0], [((1, 0), L, (2, 0)), ((0, 1), F, (1, 1))]),
        (E[1], [((-1, 0), H, (2, 0)), ((0, -1), F, (-1, -1))]),
        (E[2], [((0, 1), F, (0, 2)), ((-1, 0), F, (-1, 1))]),
        (E[3], [((0, -1), F, (0, -2)), ((1, 0), F, (1, -1))]),
    ],
    [
        (E[0], [((1, 1), L, (2, 1)), ((1, -1), L, (2, -1)), ((0, 2), F, (1, 2))]),
        (E[1], [((-1, 1), H, (2, 1)), ((-1, -1), H, (2, -1)), ((0, -2), F, (-1, -2))]),
        (E[2], [((0, 2), F, (0, 3)), ((-1, 1), F, (-1, 2))]),
        (E[3], [((0, -2), F, (0, -3)), ((1, -1), F, (1, -2))]),
    ],
    [
        (E[0], [((1, 2), L, (2, 2)), ((1, -2), L, (2, -2)), ((0, 3), F, (1, 3))]),
        (E[1], [((-1, 2), H, (2, 2)), ((-1, -2), H, (2, -2)), ((0, -3), F, (-1, -3))]),
        (E[2], [((0, 3), L, (0, 4)), ((-1, 2), F, (-1, 3))]),
        (E[3], [((0, -3), H, (0, 4)), ((1, -2), F, (1, -3))]),
    ],
    [
        (E[0], [((1, 3), L, (2, 3)), ((1, -3), L, (2, -3))]),
        (E[1], [((-1, 3), H, (2, 3)), ((-1, -3), H, (2, -3))]),
        (E[2], [((1, 3), L, (1, 4)), ((-1, 3), L, (-1, 4))]),
        (E[3], [((1, -3), H, (1, 4)), ((-1, -3), H, (-1, 4))]),
        ((1, 1), [((1, 3), F, (2, 4))]),
    ],
]


def weights_kernel(names, where, mine, ahead, *refs):
    outs, rows = refs[:-1], refs[-1]
    tokens = rows.shape[0] // len(names)
    for i, ((ox, oz), h) in enumerate(names):
        u = lax.rem(where[0] + (NX - ox), NX)
        v = lax.rem(where[1] + (NZ - oz), NZ)
        at = pl.multiple_of(((u % 2 * NZ + v) * 2 + h) * tokens, tokens)
        for k, half in enumerate((mine, ahead)):

            @pl.when(u // 2 == k)
            def _():
                rows[pl.ds(i * tokens, tokens)] = half[pl.ds(at, tokens)]

    for k, out in enumerate(outs):
        out[...] = rows[k * WORK : (k + 1) * WORK].astype(jnp.float32).T


def turned_weights(where, slices, names, tokens):
    whole = pl.BlockSpec(memory_space=pltpu.VMEM)
    count, width = len(names) * tokens, slices[0].shape[1]
    results = count // WORK
    return pl.pallas_call(
        functools.partial(weights_kernel, names),
        out_shape=[jax.ShapeDtypeStruct((width, WORK), jnp.float32)] * results,
        in_specs=[pl.BlockSpec(memory_space=pltpu.SMEM), whole, whole],
        out_specs=[whole] * results,
        scratch_shapes=[pltpu.VMEM((count, width), jnp.bfloat16)],
        compiler_params=pltpu.CompilerParams(vmem_limit_bytes=16 << 20),
        name="weights",
    )(where, *slices)


def scores_kernel(sizes, q_mine, q_other, weights, *refs):
    pieces = refs[: len(sizes)]
    out, seq, a_buf, a_sem = refs[len(sizes) :]
    queries, rows, half = q_other.shape
    count, a_copies = 0, []
    for i, (piece, size) in enumerate(zip(pieces, sizes)):
        a_copies.append(
            pltpu.make_async_copy(piece, a_buf.at[pl.ds(count, size)], a_sem.at[i])
        )
        count += size
    for copy in a_copies:
        copy.start()
    for copy in a_copies:
        copy.wait()
    total = [jnp.zeros((1, count), jnp.float32) for _ in range(queries)]
    for p, grads in enumerate((q_mine, q_other)):
        inner = lax.dot_general(
            grads[...].reshape(queries * rows, half),
            a_buf[:, :half],
            (((1,), (1,)), ((), ())),
            preferred_element_type=jnp.float32,
        )
        for q in range(queries):
            weighed = inner[q * rows : (q + 1) * rows] * weights[p * rows : (p + 1) * rows]
            total[q] = total[q] + jnp.sum(weighed, axis=0, keepdims=True)
    scores = jnp.concatenate(total + [jnp.zeros((8 - queries, count), jnp.float32)], 0)
    out[...] = scores
    ids = a_buf[:, half:].astype(jnp.float32)
    lane = lax.broadcasted_iota(jnp.int32, (count, 128), 1).astype(jnp.float32)
    onehot = jnp.where(ids == lane, 1.0, 0.0)
    seq[...] = jnp.dot(scores, onehot, precision=EXACT, preferred_element_type=jnp.float32)


def piece_scores(q_mine, q_other, weights, pieces):
    sizes = [piece.shape[0] for piece in pieces]
    count = sum(sizes)
    queries, rows, half = q_other.shape
    anywhere = pl.BlockSpec(memory_space=pl.ANY)
    whole = pl.BlockSpec(memory_space=pltpu.VMEM)
    return pl.pallas_call(
        functools.partial(scores_kernel, sizes),
        out_shape=(
            jax.ShapeDtypeStruct((8, count), jnp.float32),
            jax.ShapeDtypeStruct((8, 128), jnp.float32),
        ),
        in_specs=[whole] * 3 + [anywhere] * len(pieces),
        out_specs=[whole, whole],
        scratch_shapes=[
            pltpu.VMEM((count, half + 128), jnp.bfloat16),
            pltpu.SemaphoreType.DMA((len(pieces),)),
        ],
        compiler_params=pltpu.CompilerParams(vmem_limit_bytes=16 << 20),
        cost_estimate=pl.CostEstimate(
            flops=4 * queries * rows * half * count,
            bytes_accessed=4 * queries * rows * half + 2 * half * count,
            transcendentals=0,
        ),
        name="scores",
    )(q_mine, q_other, weights, *pieces)


def body(query_grads, out_grads, activations, seq_ids):
    queries, rows_here, width = query_grads.shape
    half = width // 2
    tokens = seq_ids.shape[0]
    rows, cols = lax.axis_size("row"), lax.axis_size("col")
    seq_count = max(tokens * rows // 32, 4)
    row, y = lax.axis_index("row"), lax.axis_index("col")
    core, z, x = lax.rem(row, 2), lax.rem(lax.div(row, 2), NZ), lax.div(row, 2 * NZ)
    where = jnp.stack([lax.rem(x + cols - y, NX), z])

    def columns(array, which):
        start = (0,) * (array.ndim - 1) + (which * half,)
        return lax.dynamic_slice(array, start, array.shape[:-1] + (half,))

    ids = jnp.broadcast_to(seq_ids[:, None], (tokens, 128)).astype(activations.dtype)
    mine = cat([columns(activations, core), ids], 1)
    other = swap(cat([columns(activations, 1 - core), ids], 1))
    own = jnp.where(core == 0, cat([mine, other]), cat([other, mine]))

    own, where, query_grads = lax.optimization_barrier((own, where, query_grads))

    q_slice = columns(query_grads, 1 - core)
    slices = cat([out_grads, swap(out_grads)], 1)
    slices, _ = lax.optimization_barrier((slices, own))
    slices = cat([slices, from_col(slices, 1, cols)])

    held = {((0, 0), h): own[h * tokens : (h + 1) * tokens] for h in F}
    order = [((0, 0), h) for h in F]
    order += [(dst, h) for moves in ROUNDS for _, load in moves for _, part, dst in load for h in part]
    slots, scores, by_seq = [], [], []
    waiting = [(own, [((0, 0), h) for h in F])]

    def work():
        count, pieces, places = 0, [], []
        while waiting and count + waiting[0][0].shape[0] <= WORK:
            piece, names = waiting.pop(0)
            pieces.append(piece)
            places.extend(names)
            count += piece.shape[0]
        part, seq = piece_scores(q_mine, q_other, weights[len(scores)], pieces)
        scores.append(part)
        by_seq.append(seq)
        slots.extend(places)

    for number, moves in enumerate(ROUNDS):
        sent = [cat([cat([held[src, h] for h in part]) for src, part, _ in load]) for _, load in moves]
        if number == 4:
            back = cat([held[(-1, -3), h] for h in F])
            sent[4] = jnp.where(core == 0, sent[4], back)
        if number == 1:
            sent, q_slice, query_grads = lax.optimization_barrier((sent, q_slice, query_grads))
            slices, q_mine = [slices, from_col(slices, 2, cols)], columns(query_grads, core)
        if number == 2:
            sent, slices, q_slice, q_mine = lax.optimization_barrier(
                (sent, slices, q_slice, q_mine)
            )
            q_other = swap(q_slice)
            weights = turned_weights(where, slices, order, tokens)
        if number == 3:
            sent, weights, q_other = lax.optimization_barrier((sent, weights, q_other))
            work()
            work()
        if number == 4:
            sent, scores = lax.optimization_barrier((sent, scores))
            work()
        for ((dx, dz), load), block in zip(moves, sent):
            came = shift(block, dx, dz, -1 if dx and dz else 1)
            names = [(dst, h) for _, part, dst in load for h in part]
            for i, name in enumerate(names):
                held[name] = came[i * tokens : (i + 1) * tokens]
            waiting.append((came, names))
    while waiting:
        work()

    partial = cat(scores, 1)[:queries]
    partial_seq = sum(by_seq[1:], by_seq[0])[:queries, :seq_count]
    far = np.array([(NX - ox, NZ - oz, h) for (ox, oz), h in slots], np.int32).T
    owner = (lax.rem(x + far[0], NX) * NZ + lax.rem(z + far[1], NZ)) * 2 + far[2]
    place = owner[:, None] == jnp.arange(rows, dtype=jnp.int32)[None, :]
    mine = jnp.einsum(
        "qst,so->oqt",
        partial.reshape(queries, rows, tokens),
        place.astype(jnp.float32),
        precision=EXACT,
    ).reshape(rows, -1)
    parts = cat(
        [mine, jnp.broadcast_to(partial_seq.reshape(1, -1), (rows, queries * seq_count))], 1
    )
    parts = jnp.broadcast_to(parts[:, None, :], (rows, cols, parts.shape[1]))
    parts = parts.reshape(rows * cols, -1)
    arrived = lax.all_to_all(parts, ("row", "col"), 0, 0, tiled=True)
    total = jnp.sum(arrived, axis=0)
    split = queries * tokens
    scores = total[:split].reshape(queries, tokens).T
    seq_scores = total[split:].reshape(queries, seq_count).T
    return (scores, seq_scores)


def solution(mesh):
    placed = (P(None, "row", "col"), P("col", "row"), P("row", "col"), P("row"))
    return jax.shard_map(
        body, mesh=mesh, in_specs=placed, out_specs=(P("row", None), P()), check_vma=False
    )
```
